32 devices in a mesh: dp: 8 (over z, x), mp: 4 (over y, core).
Axes of the slice: x: 2, y: 2, z: 4, core: 2. Of those that a mesh axis runs over, the one named last changes fastest.
Arguments:
- tokens: bfloat16 [2048, 1024], P('dp'), may hold values from -6 to 6
- segment_ids: int32 [8, 256], P('dp'), may hold values from 0 to 7, never falling along the last dimension, each value on 1 to 128 neighbouring positions
- attn_gain: float32 [1024], replicated, may hold values from 0.5 to 1.5
- w_query: bfloat16 [1024, 1024], P(None, 'mp'), may hold values from -0.1875 to 0.1875
- w_key: bfloat16 [1024, 512], P(None, 'mp'), may hold values from -0.1875 to 0.1875
- w_value: bfloat16 [1024, 512], P(None, 'mp'), may hold values from -0.1875 to 0.1875
- query_gain: float32 [64], replicated, may hold values from 0.6 to 1.4, as said below
- key_gain: float32 [64], replicated, may hold values from 0.6 to 1.4, as said below
- w_out: bfloat16 [1024, 1024], P('mp'), may hold values from -0.75 to 0.75
- ffn_gain: float32 [1024], replicated, may hold values from 0.5 to 1.5
- w_gate: bfloat16 [1024, 4608], P('dp', 'mp'), may hold values from -0.1875 to 0.1875
- w_up: bfloat16 [1024, 4608], P('dp', 'mp'), may hold values from -0.1875 to 0.1875
- w_down: bfloat16 [4608, 1024], P('mp', 'dp'), may hold values from -0.375 to 0.375
- grad_out: bfloat16 [2048, 1024], P('dp'), may hold values from -6 to 6
Outputs:
- output: bfloat16 [2048, 1024], P('dp')
- grad_tokens: float32 [2048, 1024], P('dp')
- grad_attn_gain: float32 [1024], replicated
- grad_w_query: float32 [1024, 1024], P(None, 'mp')
- grad_w_key: float32 [1024, 512], P(None, 'mp')
- grad_w_value: float32 [1024, 512], P(None, 'mp')
- grad_query_gain: float32 [64], replicated
- grad_key_gain: float32 [64], replicated
- grad_w_out: float32 [1024, 1024], P('mp')
- grad_ffn_gain: float32 [1024], replicated
- grad_w_gate: float32 [1024, 4608], P('dp', 'mp')
- grad_w_up: float32 [1024, 4608], P('dp', 'mp')
- grad_w_down: float32 [4608, 1024], P('mp', 'dp')
The draws below stay inside these ranges and needn't reach their ends.
Inputs may be any that keep to these rules, and one draw needn't show every extreme that they name: `segment_ids`: within one row the ids never fall; each row holds 8 sequences, each a run of 1 to 128 tokens, and some run has exactly 128. `query_gain`: positive scales. `key_gain`: positive scales.
All inputs are finite; a program needn't handle non-finite values.
Results may differ from the reference program's by a relative error of at most 0.015.
Values may be sent and summed in bfloat16 or wider, within the bound.
A program may use at most 128 MiB of HBM per device.

```python
import math
import jax
import jax.numpy as jnp
import numpy as np
from jax import lax

D = 1024
HEADS = 16
KV_HEADS = 8
HEAD_DIM = 64
FF = 4608
TOK_DEV = 256
MAXLEN = 128
TOKENS = 2048
N_DP = 8


def draw_query_gain(key, part):
    folded = jax.random.fold_in(key, 101)
    return jax.random.uniform(folded, (HEAD_DIM,), jnp.float32, 0.6, 1.4)


def draw_key_gain(key, part):
    folded = jax.random.fold_in(key, 202)
    return jax.random.uniform(folded, (HEAD_DIM,), jnp.float32, 0.6, 1.4)


def with_spikes(result, own_key, source, target, blocks, factor):
    def block_of(dim):
        return (jnp.arange(result.shape[dim]) // (result.shape[dim] // blocks)).reshape((-1,) + (1,) * (result.ndim - 1 - dim))

    one_side = jax.random.permutation(own_key, blocks)[block_of(target)]
    second = (block_of(target) + blocks // 2) % blocks
    return jnp.where((block_of(source) == one_side) | (block_of(source) == second), factor * result, result)


def level_of(stream_key, shape, shards, low, high):
    loudness, own = 1.0, jax.random.fold_in(stream_key, 6)
    for dim, shards_of in shards:
        draws = jnp.exp(jax.random.uniform(jax.random.fold_in(own, dim), (shards_of,), jnp.float32, low / len(shards), high / len(shards)))
        loudness = loudness * jnp.repeat(draws, shape[dim] // shards_of).reshape([-1 if axis == dim else 1 for axis in range(len(shape))])
    return loudness


def length_profile(amount, total, reach, lean):
    portions = [(1 << 20) // math.isqrt(rank ** lean) + 1 for rank in range(2, amount + 1)]
    spare, counts = total - reach - (amount - 1), [1] * (amount - 1)
    while spare > 0:
        candidates = [i for i in range(amount - 1) if counts[i] < reach]
        whole, budget = sum([portions[i] for i in candidates]), spare
        for i in candidates:
            extra = min(reach - counts[i], max(1, budget * portions[i] // whole), spare)
            counts[i] = counts[i] + extra
            spare = spare - extra
    return np.array([reach] + counts)


def uneven(stream_key, count, total, limit, slope):
    if count == 2:
        one = jax.random.randint(stream_key, (), max(1, total - limit), min(limit, total - 1) + 1)
        return jnp.stack([one, total - one])
    sizes = jnp.asarray(length_profile(count, total, limit, slope), jnp.int32)
    couples = (count - 1) // 2
    donor, taker = sizes[1:1 + 2 * couples:2], sizes[2:2 + 2 * couples:2]
    room = jnp.minimum(donor - 1, limit - taker)
    moved = jax.random.randint(jax.random.fold_in(stream_key, 1), (couples,), 0, 1 << 20) % (room + 1)
    sizes = sizes.at[1:1 + 2 * couples:2].set(donor - moved).at[2:2 + 2 * couples:2].set(taker + moved)
    return sizes[jax.random.permutation(jax.random.fold_in(stream_key, 2), count)]


def noise(stream_key, extent, spread, most, shards=(), kind=jnp.bfloat16):
    level = level_of(stream_key, extent, shards, -0.22, 0.18) if shards else 1.0
    result = jax.random.normal(stream_key, extent, jnp.float32) * spread * level
    return jnp.minimum(jnp.maximum(result, -most), most).astype(kind)


def gaussian_with(own_key, extent, deviation, reach, shards, heavy, held_as=jnp.bfloat16):
    values = deviation * jax.random.normal(own_key, extent, jnp.float32)
    if shards:
        values = values * level_of(own_key, extent, shards, -0.22, 0.18)
    return jnp.clip(with_spikes(values, jax.random.fold_in(own_key, 3), *heavy), -reach, reach).astype(held_as)


def setup_inputs(seed: int = 0) -> dict:
    arg_keys = jax.random.split(jax.random.key(seed), 15)
    tokens = noise(arg_keys[0], (TOKENS, D), 1.0, 6.0, ((0, 8),))
    segment_ids = jax.vmap(lambda own: jnp.searchsorted(jnp.cumsum(uneven(own, 8, TOK_DEV, MAXLEN, 2)), jnp.arange(TOK_DEV), side="right"))(jax.random.split(arg_keys[1], N_DP)).reshape((N_DP, TOK_DEV)).astype(jnp.int32)
    attn_gain = jnp.clip(1.0 + 0.1 * jax.random.normal(arg_keys[2], (D,), jnp.float32), 0.5, 1.5)
    w_query = noise(arg_keys[3], (D, HEADS * HEAD_DIM), D ** -0.5, 0.1875, ((1, 4),))
    w_key = noise(arg_keys[4], (D, KV_HEADS * HEAD_DIM), D ** -0.5, 0.1875, ((1, 4),))
    w_value = noise(arg_keys[5], (D, KV_HEADS * HEAD_DIM), D ** -0.5, 0.1875, ((1, 4),))
    query_gain = draw_query_gain(jax.random.fold_in(arg_keys[14], 71), 0)
    key_gain = draw_key_gain(jax.random.fold_in(arg_keys[14], 71), 0)
    w_out = noise(arg_keys[8], (HEADS * HEAD_DIM, D), HEAD_DIM ** -0.5, 0.75, ((0, 4),))
    ffn_gain = jnp.clip(1.0 + 0.1 * jax.random.normal(arg_keys[9], (D,), jnp.float32), 0.5, 1.5)
    w_gate = noise(arg_keys[10], (D, FF), D ** -0.5, 0.1875, ((0, 8), (1, 4)))
    w_up = noise(arg_keys[11], (D, FF), D ** -0.5, 0.1875, ((0, 8), (1, 4)))
    w_down = noise(arg_keys[12], (FF, D), (FF // 16) ** -0.5, 0.375, ((0, 4), (1, 8)))
    grad_out = gaussian_with(arg_keys[13], (TOKENS, D), 1.0, 6.0, ((0, 8),), (0, 1, 8, 2.0))
    return dict(tokens=tokens, segment_ids=segment_ids, attn_gain=attn_gain, w_query=w_query, w_key=w_key, w_value=w_value, query_gain=query_gain, key_gain=key_gain, w_out=w_out, ffn_gain=ffn_gain, w_gate=w_gate, w_up=w_up, w_down=w_down, grad_out=grad_out)


EPS = 1e-05
ROPE_BASE = 1000000.0

def rms_scale(values):
    return lax.rsqrt(lax.optimization_barrier(jnp.mean(values * values, axis=-1, keepdims=True)) + EPS)

def norm_back(values, scale_fac, gain_vec, grad_normed):
    weighted = grad_normed * gain_vec
    grad_values = scale_fac * weighted - values * scale_fac * scale_fac * scale_fac * lax.optimization_barrier(jnp.mean(weighted * values, axis=-1, keepdims=True))
    grad_gain = lax.optimization_barrier(jnp.sum((grad_normed * values * scale_fac).reshape(-1, values.shape[-1]), axis=0))
    return (grad_values, grad_gain)

def segment_layout(segment_row):
    token_count = segment_row.shape[0]
    token_index = jnp.arange(token_count, dtype=jnp.int32)
    same_doc = segment_row[:, None] == segment_row[None, :]
    starts = lax.optimization_barrier(jnp.min(jnp.where(same_doc, token_index[None, :], token_count), axis=1)).astype(jnp.int32)
    allowed = same_doc & (token_index[None, :] <= token_index[:, None])
    return ((token_index - starts).astype(jnp.float32), allowed)

def rotary_tables(position, head_width):
    half_index = jnp.arange(head_width // 2, dtype=jnp.float32)
    frequency = ROPE_BASE ** (-2.0 * half_index / head_width)
    angles = position[:, None] * frequency[None, :]
    return (jnp.cos(angles)[:, None, :], jnp.sin(angles)[:, None, :])

def rotate(values, cosine, sine_table):
    half_width = values.shape[-1] // 2
    front_part = values[..., :half_width]
    back_part = values[..., half_width:]
    return jnp.concatenate([front_part * cosine - back_part * sine_table, back_part * cosine + front_part * sine_table], axis=-1)

def rotate_back(grads_in, cosine, sine_table):
    half_width = grads_in.shape[-1] // 2
    front_part = grads_in[..., :half_width]
    back_part = grads_in[..., half_width:]
    return jnp.concatenate([front_part * cosine + back_part * sine_table, back_part * cosine - front_part * sine_table], axis=-1)

def masked_scores(query_rot, key_rot, allowed):
    token_count, head_count, head_width = query_rot.shape
    group_count = key_rot.shape[1]
    grouped = query_rot.reshape(token_count, group_count, head_count // group_count, head_width).astype(jnp.float32)
    scores = jnp.einsum('qgrd,kgd->grqk', grouped, key_rot.astype(jnp.float32)) * (1.0 / math.sqrt(head_width))
    return (jnp.where(allowed, scores, -1e+30), grouped)

def attention_forward(query_rot, key_rot, value_half, allowed):
    token_count, head_count, head_width = query_rot.shape
    scores, grouped = masked_scores(query_rot, key_rot, allowed)
    row_peak = lax.optimization_barrier(jnp.max(scores, axis=-1, keepdims=True))
    raised = jnp.exp(scores - row_peak)
    row_total = lax.optimization_barrier(jnp.sum(raised, axis=-1, keepdims=True))
    logsum = row_peak + jnp.log(row_total)
    prob_half = (raised / row_total).astype(jnp.bfloat16)
    attended = jnp.einsum('grqk,kgd->qgrd', prob_half.astype(jnp.float32), value_half.astype(jnp.float32)).astype(jnp.bfloat16)
    return (attended.reshape(token_count, head_count, head_width), logsum)

def attention_backward(query_rot, key_rot, value_half, allowed, attended, logsum, d_attended):
    token_count, head_count, head_width = query_rot.shape
    group_count = key_rot.shape[1]
    scores, grouped = masked_scores(query_rot, key_rot, allowed)
    probs = jnp.where(allowed, jnp.exp(scores - logsum), 0.0)
    prob_half = probs.astype(jnp.bfloat16).astype(jnp.float32)
    d_grouped = d_attended.reshape(token_count, group_count, head_count // group_count, head_width).astype(jnp.float32)
    d_value = jnp.einsum('grqk,qgrd->kgd', prob_half, d_grouped).astype(jnp.bfloat16)
    d_probs = jnp.einsum('qgrd,kgd->grqk', d_grouped, value_half.astype(jnp.float32))
    row_delta = lax.optimization_barrier(jnp.sum(d_attended.astype(jnp.float32) * attended.astype(jnp.float32), axis=-1))
    row_delta = row_delta.reshape(token_count, group_count, head_count // group_count).transpose(1, 2, 0)[..., None]
    d_scores = (probs * (d_probs - row_delta) * (1.0 / math.sqrt(head_width))).astype(jnp.bfloat16).astype(jnp.float32)
    d_query_rot = jnp.einsum('grqk,kgd->qgrd', d_scores, key_rot.astype(jnp.float32)).reshape(token_count, head_count, head_width)
    d_key_rot = jnp.einsum('grqk,qgrd->kgd', d_scores, grouped)
    return (d_query_rot, d_key_rot, d_value)

def layer_block(params_all, token_blk, segment_row, grad_blk):
    attn_gain, w_query, w_key, w_value, query_gain, key_gain, w_out, ffn_gain, w_gate, w_up, w_down = params_all
    token_count = token_blk.shape[0]
    inputs = token_blk.astype(jnp.float32)
    scale_in = rms_scale(inputs)
    normed_in = (inputs * scale_in * attn_gain).astype(jnp.bfloat16)
    query_proj = jnp.dot(normed_in, w_query, preferred_element_type=jnp.float32).reshape(token_count, -1, HEAD_DIM)
    key_proj = jnp.dot(normed_in, w_key, preferred_element_type=jnp.float32).reshape(token_count, -1, HEAD_DIM)
    value_half = jnp.dot(normed_in, w_value, preferred_element_type=jnp.float32).astype(jnp.bfloat16).reshape(token_count, -1, HEAD_DIM)
    query_scale = rms_scale(query_proj)
    key_scale = rms_scale(key_proj)
    position, allowed = segment_layout(segment_row)
    cosine, sine_table = rotary_tables(position, HEAD_DIM)
    query_rot = rotate(query_proj * query_scale * query_gain, cosine, sine_table).astype(jnp.bfloat16)
    key_rot = rotate(key_proj * key_scale * key_gain, cosine, sine_table).astype(jnp.bfloat16)
    attended, logsum = attention_forward(query_rot, key_rot, value_half, allowed)
    attn_flat = attended.reshape(token_count, -1)
    hidden = inputs + jnp.dot(attn_flat, w_out, preferred_element_type=jnp.float32)
    scale_mid = rms_scale(hidden)
    normed_mid = (hidden * scale_mid * ffn_gain).astype(jnp.bfloat16)
    gate_proj = jnp.dot(normed_mid, w_gate, preferred_element_type=jnp.float32)
    up_proj = jnp.dot(normed_mid, w_up, preferred_element_type=jnp.float32)
    sig_gate = jax.nn.sigmoid(gate_proj)
    activated = (gate_proj * sig_gate * up_proj).astype(jnp.bfloat16)
    output = (hidden + jnp.dot(activated, w_down, preferred_element_type=jnp.float32)).astype(jnp.bfloat16)
    d_act = jnp.dot(grad_blk, w_down.T, preferred_element_type=jnp.float32)
    d_up = (d_act * gate_proj * sig_gate).astype(jnp.bfloat16)
    d_gate = (d_act * up_proj * sig_gate * (1.0 + gate_proj * (1.0 - sig_gate))).astype(jnp.bfloat16)
    g_gate = jnp.dot(normed_mid.T, d_gate, preferred_element_type=jnp.float32)
    g_up = jnp.dot(normed_mid.T, d_up, preferred_element_type=jnp.float32)
    g_down = jnp.dot(activated.T, grad_blk, preferred_element_type=jnp.float32)
    d_mid = jnp.dot(d_gate, w_gate.T, preferred_element_type=jnp.float32) + jnp.dot(d_up, w_up.T, preferred_element_type=jnp.float32)
    d_hidden_norm, g_ffn_gain = norm_back(hidden, scale_mid, ffn_gain, d_mid)
    d_hidden = grad_blk.astype(jnp.float32) + d_hidden_norm
    d_hidden_half = d_hidden.astype(jnp.bfloat16)
    g_out = jnp.dot(attn_flat.T, d_hidden_half, preferred_element_type=jnp.float32)
    d_attended = jnp.dot(d_hidden_half, w_out.T, preferred_element_type=jnp.float32).astype(jnp.bfloat16).reshape(token_count, -1, HEAD_DIM)
    d_query_rot, d_key_rot, d_value = attention_backward(query_rot, key_rot, value_half, allowed, attended, logsum, d_attended)
    d_query, g_query_gain = norm_back(query_proj, query_scale, query_gain, rotate_back(d_query_rot, cosine, sine_table))
    d_key, g_key_gain = norm_back(key_proj, key_scale, key_gain, rotate_back(d_key_rot, cosine, sine_table))
    d_query_half = d_query.astype(jnp.bfloat16).reshape(token_count, -1)
    d_key_half = d_key.astype(jnp.bfloat16).reshape(token_count, -1)
    d_value_half = d_value.reshape(token_count, -1)
    g_query = jnp.dot(normed_in.T, d_query_half, preferred_element_type=jnp.float32)
    g_key = jnp.dot(normed_in.T, d_key_half, preferred_element_type=jnp.float32)
    g_value = jnp.dot(normed_in.T, d_value_half, preferred_element_type=jnp.float32)
    d_in = jnp.dot(d_query_half, w_query.T, preferred_element_type=jnp.float32)
    d_in = d_in + jnp.dot(d_key_half, w_key.T, preferred_element_type=jnp.float32)
    d_in = d_in + jnp.dot(d_value_half, w_value.T, preferred_element_type=jnp.float32)
    d_in_norm, g_attn_gain = norm_back(inputs, scale_in, attn_gain, d_in)
    grad_tokens = d_hidden + d_in_norm
    block_grads = (g_attn_gain, g_query, g_key, g_value, g_query_gain, g_key_gain, g_out, g_ffn_gain, g_gate, g_up, g_down)
    return (output, grad_tokens, block_grads)

def reference(tokens, segment_ids, attn_gain, w_query, w_key, w_value, query_gain, key_gain, w_out, ffn_gain, w_gate, w_up, w_down, grad_out):
    params_all = (attn_gain, w_query, w_key, w_value, query_gain, key_gain, w_out, ffn_gain, w_gate, w_up, w_down)
    token_blocks = tokens.reshape(N_DP, TOK_DEV, D)
    grad_blocks = grad_out.reshape(N_DP, TOK_DEV, D)
    zero_grads = tuple((jnp.zeros(weight_arr.shape, jnp.float32) for weight_arr in params_all))

    def one_block(carried, blk_inputs):
        token_blk, segment_row, grad_blk = blk_inputs
        output, grad_tokens, block_grads = layer_block(params_all, token_blk, segment_row, grad_blk)
        summed = tuple((old_grad + new_grad for old_grad, new_grad in zip(carried, block_grads)))
        return (summed, (output, grad_tokens))
    totals, (outputs, grad_rows) = lax.scan(one_block, zero_grads, (token_blocks, segment_ids, grad_blocks))
    return (outputs.reshape(TOKENS, D), grad_rows.reshape(TOKENS, D), totals[0], totals[1], totals[2], totals[3], totals[4], totals[5], totals[6], totals[7], totals[8], totals[9], totals[10])
```

```python
import functools
import math

import jax
import jax.numpy as jnp
from jax import lax
from jax.experimental import pallas as pl
from jax.experimental.pallas import tpu as pltpu
from jax.sharding import PartitionSpec as P

HEAD_DIM = 64


EPS = 1e-05
ROPE_BASE = 1000000.0


def rms_scale(values):
    return lax.rsqrt(jnp.mean(values * values, axis=-1, keepdims=True) + EPS)


def norm_back(values, scale_fac, gain_vec, grad_normed):
    weighted = grad_normed * gain_vec
    grad_values = scale_fac * weighted - values * scale_fac * scale_fac * scale_fac * jnp.mean(
        weighted * values, axis=-1, keepdims=True
    )
    grad_gain = jnp.sum((grad_normed * values * scale_fac).reshape(-1, values.shape[-1]), axis=0)
    return (grad_values, grad_gain)


def segment_layout(segment_row):
    token_count = segment_row.shape[0]
    token_index = jnp.arange(token_count, dtype=jnp.int32)
    same_doc = segment_row[:, None] == segment_row[None, :]
    starts = jnp.min(jnp.where(same_doc, token_index[None, :], token_count), axis=1)
    allowed = same_doc & (token_index[None, :] <= token_index[:, None])
    return ((token_index - starts).astype(jnp.float32), allowed)


def rotary_tables(position, head_width):
    half_index = jnp.arange(head_width // 2, dtype=jnp.float32)
    frequency = ROPE_BASE ** (-2.0 * half_index / head_width)
    angles = position[:, None] * frequency[None, :]
    return (jnp.cos(angles)[:, None, :], jnp.sin(angles)[:, None, :])


def rotate(values, cosine, sine_table):
    half_width = values.shape[-1] // 2
    front_part = values[..., :half_width]
    back_part = values[..., half_width:]
    return jnp.concatenate(
        [
            front_part * cosine - back_part * sine_table,
            back_part * cosine + front_part * sine_table,
        ],
        axis=-1,
    )


def rotate_back(grads_in, cosine, sine_table):
    half_width = grads_in.shape[-1] // 2
    front_part = grads_in[..., :half_width]
    back_part = grads_in[..., half_width:]
    return jnp.concatenate(
        [
            front_part * cosine + back_part * sine_table,
            back_part * cosine - front_part * sine_table,
        ],
        axis=-1,
    )


def masked_scores(query_rot, key_rot, allowed):
    token_count, head_count, head_width = query_rot.shape
    group_count = key_rot.shape[1]
    grouped = query_rot.reshape(token_count, group_count, head_count // group_count, head_width)
    scores = jnp.einsum("qgrd,kgd->grqk", grouped, key_rot, preferred_element_type=jnp.float32) * (
        1.0 / math.sqrt(head_width)
    )
    return (jnp.where(allowed, scores, -1e30), grouped)


def attention_forward(query_rot, key_rot, value_half, allowed):
    token_count, head_count, head_width = query_rot.shape
    scores, grouped = masked_scores(query_rot, key_rot, allowed)
    row_peak = jnp.max(scores, axis=-1, keepdims=True)
    raised = jnp.exp(scores - row_peak)
    row_total = jnp.sum(raised, axis=-1, keepdims=True)
    logsum = row_peak + jnp.log(row_total)
    prob_half = (raised / row_total).astype(jnp.bfloat16)
    attended = jnp.einsum(
        "grqk,kgd->qgrd", prob_half, value_half, preferred_element_type=jnp.float32
    ).astype(jnp.bfloat16)
    return (attended.reshape(token_count, head_count, head_width), logsum)


def attention_backward(query_rot, key_rot, value_half, allowed, attended, logsum, d_attended):
    token_count, head_count, head_width = query_rot.shape
    group_count = key_rot.shape[1]
    scores, grouped = masked_scores(query_rot, key_rot, allowed)
    probs = jnp.where(allowed, jnp.exp(scores - logsum), 0.0)
    prob_half = probs.astype(jnp.bfloat16)
    d_grouped = d_attended.reshape(token_count, group_count, head_count // group_count, head_width)
    d_value = jnp.einsum(
        "grqk,qgrd->kgd", prob_half, d_grouped, preferred_element_type=jnp.float32
    ).astype(jnp.bfloat16)
    d_probs = jnp.einsum(
        "qgrd,kgd->grqk", d_grouped, value_half, preferred_element_type=jnp.float32
    )
    row_delta = jnp.sum(d_attended.astype(jnp.float32) * attended.astype(jnp.float32), axis=-1)
    row_delta = row_delta.reshape(token_count, group_count, head_count // group_count).transpose(
        1, 2, 0
    )[..., None]
    d_scores = (probs * (d_probs - row_delta) * (1.0 / math.sqrt(head_width))).astype(jnp.bfloat16)
    d_query_rot = jnp.einsum(
        "grqk,kgd->qgrd", d_scores, key_rot, preferred_element_type=jnp.float32
    ).reshape(token_count, head_count, head_width)
    d_key_rot = jnp.einsum("grqk,qgrd->kgd", d_scores, grouped, preferred_element_type=jnp.float32)
    return (d_query_rot, d_key_rot, d_value)


RING_LIMIT = 16


def ring_order(count):
    return tuple(range(0, count, 2)) + tuple(range(count - 1, 0, -2))


def ring_moves(count):
    order = ring_order(count)
    ahead = [(order[i], order[(i + 1) % count]) for i in range(count)]
    back = [(order[(i + 1) % count], order[i]) for i in range(count)]
    return ahead, back


def ring_place(count):
    order = ring_order(count)
    place = [0] * count
    for spot, owner in enumerate(order):
        place[owner] = spot
    me = jnp.array(place, dtype=jnp.int32)[lax.axis_index("dp")]
    table = jnp.array(order, dtype=jnp.int32)
    return lambda step: table[(me + step + 2 * count) % count]


class Gather:
    def __init__(self, block, count):
        self.count, self.block = count, block
        self.ring = count >= 4 and count % 2 == 0 and count <= RING_LIMIT
        self.left = self.right = block
        self.done = 0
        if self.ring:
            self.owner = ring_place(count)
            self.moves = ring_moves(count)
            self.whole = None

    def put(self, piece, who, shift=0):
        start = who * self.block.shape[0] + shift
        self.whole = lax.dynamic_update_slice_in_dim(self.whole, piece, start, 0)

    def step(self):
        if not self.ring or self.done >= self.count // 2:
            return
        self.done += 1
        ahead, back = self.moves
        half = self.block.shape[0] // 2
        if self.done < self.count // 2:
            self.left = lax.ppermute(self.left, "dp", ahead)
            self.right = lax.ppermute(self.right, "dp", back)
            if self.whole is None:
                zero, self.left, self.right = lax.optimization_barrier(
                    (jnp.zeros((), self.block.dtype), self.left, self.right)
                )
                self.whole = jnp.broadcast_to(
                    zero, (self.count * self.block.shape[0],) + self.block.shape[1:]
                )
                self.put(self.block, self.owner(0))
            self.put(self.left, self.owner(-self.done))
            self.put(self.right, self.owner(self.done))
        else:
            far = self.owner(self.done)
            self.put(lax.ppermute(self.left[:half], "dp", ahead), far)
            self.put(lax.ppermute(self.right[half:], "dp", back), far, half)

    def tie(self, value):
        if not self.ring:
            return value
        value, self.left, self.right = lax.optimization_barrier((value, self.left, self.right))
        self.step()
        return value

    def result(self):
        if self.count == 1:
            return self.block
        if not self.ring:
            return lax.all_gather(self.block, "dp", axis=0, tiled=True)
        while self.done < self.count // 2:
            self.step()
        return self.whole


class Scatter:
    def __init__(self, terms, count):
        self.count, self.terms = count, terms
        self.ring = count >= 4 and count % 2 == 0 and count <= RING_LIMIT
        if not self.ring:
            return
        self.rows = terms.shape[0] // count
        self.owner = ring_place(count)
        self.moves = ring_moves(count)
        self.left = count // 2
        half = self.rows // 2
        self.cw = self.term(self.left, 0, half)
        self.ccw = self.term(self.left, half, half)
        self.send()

    def term(self, step, start=0, size=None):
        return lax.dynamic_slice_in_dim(
            self.terms, self.owner(step) * self.rows + start, size or self.rows, 0
        )

    def plus(self, one, two):
        return (one.astype(jnp.float32) + two.astype(jnp.float32)).astype(self.terms.dtype)

    def send(self):
        self.cw = lax.ppermute(self.cw, "dp", self.moves[0])
        self.ccw = lax.ppermute(self.ccw, "dp", self.moves[1])
        self.left -= 1

    def step(self):
        if not self.ring or self.left == 0:
            return
        step, half = self.left, self.rows // 2
        if step == self.count // 2 - 1:
            self.cw = jnp.concatenate(
                [self.plus(self.term(step, 0, half), self.cw), self.term(step, half, half)], axis=0
            )
            self.ccw = jnp.concatenate(
                [self.term(-step, 0, half), self.plus(self.term(-step, half, half), self.ccw)],
                axis=0,
            )
        else:
            self.cw = self.plus(self.term(step), self.cw)
            self.ccw = self.plus(self.term(-step), self.ccw)
        self.send()

    def finished(self, value):
        if not self.ring:
            return value
        while self.left:
            self.step()
        value, self.cw, self.ccw = lax.optimization_barrier((value, self.cw, self.ccw))
        return value

    def tie(self, value):
        if not self.ring or self.left == 0:
            return value
        value, self.cw, self.ccw = lax.optimization_barrier((value, self.cw, self.ccw))
        self.step()
        return value

    def result(self):
        if self.count == 1:
            return self.terms.astype(jnp.float32)
        if not self.ring:
            total = lax.psum_scatter(self.terms, "dp", scatter_dimension=0, tiled=True)
            return total.astype(jnp.float32)
        while self.left:
            self.step()
        own = self.term(0).astype(jnp.float32)
        return own + self.cw.astype(jnp.float32) + self.ccw.astype(jnp.float32)


def sum_all(vector, sizes):
    for name, count in sizes:
        if count & (count - 1) or count > RING_LIMIT:
            vector = lax.psum(vector, name)
            continue
        reach = 1
        while reach < count:
            pairs = [(i, i ^ reach) for i in range(count)]
            vector = vector + lax.ppermute(vector, name, pairs)
            reach *= 2
    return vector


def sum_heads(part, count, tie=lambda value: value):
    if count != 4:
        return lax.psum(part, "mp")
    near = [(i, i ^ 1) for i in range(count)]
    across = [(i, i ^ 2) for i in range(count)]
    half = part.shape[0] // 2
    bit = lax.axis_index("mp") % 2
    kept = lax.dynamic_slice_in_dim(part, bit * half, half, 0)
    given = lax.dynamic_slice_in_dim(part, (1 - bit) * half, half, 0).astype(jnp.bfloat16)
    mine = kept + lax.ppermute(given, "mp", near).astype(jnp.float32)
    mine = tie(lax.reduce_precision(mine, 8, 7))
    other = lax.ppermute(mine.astype(jnp.bfloat16), "mp", across)
    mine = mine + other.astype(jnp.float32)
    other = lax.ppermute(mine, "mp", near)
    return jnp.where(
        bit == 0,
        jnp.concatenate([mine, other], axis=0),
        jnp.concatenate([other, mine], axis=0),
    )


MESH_ID = pl.DeviceIdType.MESH


def finish_kernel(
    count,
    terms,
    part,
    vector,
    grads,
    total,
    gains,
    cw_in,
    ccw_in,
    cw_out,
    ccw_out,
    near_out,
    near_in,
    far_out,
    far_in,
    vec_out,
    vec_in,
    ring_send,
    ring_recv,
    pair_send,
    pair_recv,
    vec_send,
    vec_recv,
):
    dp, mp = lax.axis_index("dp"), lax.axis_index("mp")
    rows = terms.shape[0] // count
    half = rows // 2
    far = count // 2

    def owner(spot):
        spot = lax.rem(spot + 2 * count, count)
        low = 1 - spot // far
        return low * 2 * spot + (1 - low) * (2 * (count - spot) - 1)

    odd = lax.rem(dp, 2)
    place = (1 - odd) * (dp // 2) + odd * (count - (dp + 1) // 2)
    ahead, behind = (owner(place + 1), mp), (owner(place - 1), mp)

    def pair(value, reach):
        return value + reach * (1 - 2 * lax.rem(value // reach, 2))

    partners = [(dp, pair(mp, 1)), (dp, pair(mp, 2))]
    reach = 1
    while reach < count:
        partners.append((pair(dp, reach), mp))
        reach *= 2

    barrier = pltpu.get_barrier_semaphore()
    for target in [ahead, behind] + partners:
        pl.semaphore_signal(barrier, inc=1, device_id=target, device_id_type=MESH_ID)
    pl.semaphore_wait(barrier, 2 + len(partners))

    def send(source, dest, sems, target):
        copy = pltpu.make_async_remote_copy(
            src_ref=source,
            dst_ref=dest,
            send_sem=sems[0],
            recv_sem=sems[1],
            device_id=target,
            device_id_type=MESH_ID,
        )
        copy.start()
        return copy

    def rows_of(spot, start=0, size=None):
        return pl.ds(pl.multiple_of(owner(place + spot) * rows + start, 16), size or rows)

    def term(spot, start=0, size=None):
        return terms[rows_of(spot, start, size), :].astype(jnp.float32)

    def ring_sems(way, turn):
        return ring_send.at[way, turn], ring_recv.at[way, turn]

    cw = send(
        terms.at[rows_of(far, 0, half), :], cw_in.at[0, pl.ds(0, half)], ring_sems(0, 0), ahead
    )
    ccw = send(
        terms.at[rows_of(-far, half, half), :],
        ccw_in.at[0, pl.ds(half, half)],
        ring_sems(1, 0),
        behind,
    )

    bit = lax.rem(mp, 2)
    middle = part.shape[0] // 2
    kept = pl.ds(pl.multiple_of(bit * middle, 16), middle)
    given = pl.ds(pl.multiple_of((1 - bit) * middle, 16), middle)
    near_out[...] = part[given, :].astype(jnp.bfloat16)
    pairs = [send(near_out, near_in, (pair_send.at[0], pair_recv.at[0]), partners[0])]

    vec_out[0] = vector[...]
    vecs = [send(vec_out.at[0], vec_in.at[0], (vec_send.at[0], vec_recv.at[0]), partners[0])]

    def vector_turn():
        turn = len(vecs) - 1
        if turn >= len(partners):
            return
        vecs[turn].wait()
        both = vec_out[turn] + vec_in[turn]
        if turn + 1 == len(partners):
            gains[...] = both
            vecs.append(None)
            return
        vec_out[turn + 1] = both
        sems = (vec_send.at[turn + 1], vec_recv.at[turn + 1])
        vecs.append(send(vec_out.at[turn + 1], vec_in.at[turn + 1], sems, partners[turn + 1]))

    def pair_turn():
        turn = len(pairs)
        if turn == 1:
            pairs[0].wait()
            far_out[...] = (part[kept, :] + near_in[...].astype(jnp.float32)).astype(jnp.bfloat16)
            pairs.append(send(far_out, far_in, (pair_send.at[1], pair_recv.at[1]), partners[1]))
        elif turn == 2:
            pairs[1].wait()
            total[kept, :] = far_out[...].astype(jnp.float32) + far_in[...].astype(jnp.float32)
            view = total.at[kept, :]
            pairs.append(send(view, view, (pair_send.at[2], pair_recv.at[2]), partners[0]))
        elif turn == 3:
            pairs[2].wait()
            pairs.append(None)

    for turn in range(1, far):
        spot = far - turn
        cw.wait()
        if turn == 1:
            low, high = pl.ds(0, half), pl.ds(half, half)
            cw_out[0, low] = (term(spot, 0, half) + cw_in[0, low].astype(jnp.float32)).astype(
                jnp.bfloat16
            )
            cw_out[0, high] = terms[rows_of(spot, half, half), :]
        else:
            cw_out[turn - 1] = (term(spot) + cw_in[turn - 1].astype(jnp.float32)).astype(
                jnp.bfloat16
            )
        cw = send(cw_out.at[turn - 1], cw_in.at[turn], ring_sems(0, turn), ahead)
        ccw.wait()
        if turn == 1:
            ccw_out[0, high] = (
                term(-spot, half, half) + ccw_in[0, high].astype(jnp.float32)
            ).astype(jnp.bfloat16)
            ccw_out[0, low] = terms[rows_of(-spot, 0, half), :]
        else:
            ccw_out[turn - 1] = (term(-spot) + ccw_in[turn - 1].astype(jnp.float32)).astype(
                jnp.bfloat16
            )
        ccw = send(ccw_out.at[turn - 1], ccw_in.at[turn], ring_sems(1, turn), behind)
        pair_turn()
        vector_turn()
    cw.wait()
    ccw.wait()
    own = term(0) + cw_in[far - 1].astype(jnp.float32) + ccw_in[far - 1].astype(jnp.float32)
    grads[rows_of(0), :] = own.astype(jnp.bfloat16)

    for turn in range(1, far + 1):
        size = rows if turn < far else half
        shift = 0 if turn < far else half
        one = grads.at[rows_of(1 - turn, 0, size), :]
        two = grads.at[rows_of(turn - 1, shift, size), :]
        cw = send(one, one, ring_sems(0, far + turn - 1), ahead)
        ccw = send(two, two, ring_sems(1, far + turn - 1), behind)
        pair_turn()
        vector_turn()
        cw.wait()
        ccw.wait()
    while len(pairs) < 4:
        pair_turn()
    while len(vecs) <= len(partners):
        vector_turn()


def finish(terms, part, vector, dp_count):
    rows, columns = terms.shape[0] // dp_count, terms.shape[1]
    far, steps = dp_count // 2, 2 + dp_count.bit_length() - 1
    lanes = 128
    tall = -(-vector.shape[0] // (8 * lanes)) * 8
    padded = jnp.pad(vector, (0, tall * lanes - vector.shape[0])).reshape(tall, lanes)
    middle = (part.shape[0] // 2, part.shape[1])
    ring_slots = pltpu.VMEM((far, rows, columns), jnp.bfloat16)
    half_slot = pltpu.VMEM(middle, jnp.bfloat16)
    vec_slots = pltpu.VMEM((steps, tall, lanes), jnp.float32)
    vmem = pl.BlockSpec(memory_space=pltpu.VMEM)
    grads, total, gains = pl.pallas_call(
        functools.partial(finish_kernel, dp_count),
        out_shape=(
            jax.ShapeDtypeStruct(terms.shape, jnp.bfloat16),
            jax.ShapeDtypeStruct(part.shape, jnp.float32),
            jax.ShapeDtypeStruct(padded.shape, jnp.float32),
        ),
        in_specs=[vmem] * 3,
        out_specs=(vmem,) * 3,
        scratch_shapes=[ring_slots] * 4
        + [half_slot] * 4
        + [vec_slots] * 2
        + [pltpu.SemaphoreType.DMA((2, 2 * far))] * 2
        + [pltpu.SemaphoreType.DMA((3,))] * 2
        + [pltpu.SemaphoreType.DMA((steps,))] * 2,
        compiler_params=pltpu.CompilerParams(
            collective_id=0, has_side_effects=True, vmem_limit_bytes=24 * 1024 * 1024
        ),
    )(terms, part, padded)
    return grads, total, gains.reshape(-1)[: vector.shape[0]]


def shards(
    dp_count,
    mp_count,
    tokens,
    segment_ids,
    attn_gain,
    w_query,
    w_key,
    w_value,
    query_gain,
    key_gain,
    w_out,
    ffn_gain,
    w_gate,
    w_up,
    w_down,
    grad_out,
):
    token_count, width = tokens.shape
    across = (((1,), (1,)), ((), ()))
    down_rows = (((0,), (0,)), ((), ()))
    mid_width = w_gate.shape[1]
    block = jnp.concatenate([w_gate, w_up, w_down.T], axis=1)
    tokens, block = lax.optimization_barrier((tokens, block))
    ring = Gather(block, dp_count)
    ring.step()
    w_heads = jnp.concatenate([w_query, w_key, w_value], axis=1)
    query_width, key_width = w_query.shape[1], w_key.shape[1]
    inputs = tokens.astype(jnp.float32)
    scale_in = rms_scale(inputs)
    normed_in = (inputs * scale_in * attn_gain).astype(jnp.bfloat16)
    heads_proj = jnp.dot(normed_in, w_heads, preferred_element_type=jnp.float32)
    query_proj = heads_proj[:, :query_width].reshape(token_count, -1, HEAD_DIM)
    key_proj = heads_proj[:, query_width : query_width + key_width].reshape(
        token_count, -1, HEAD_DIM
    )
    value_half = (
        heads_proj[:, query_width + key_width :]
        .astype(jnp.bfloat16)
        .reshape(token_count, -1, HEAD_DIM)
    )
    query_scale = rms_scale(query_proj)
    key_scale = rms_scale(key_proj)
    position, allowed = segment_layout(segment_ids[0])
    cosine, sine_table = rotary_tables(position, HEAD_DIM)
    query_rot = rotate(query_proj * query_scale * query_gain, cosine, sine_table).astype(
        jnp.bfloat16
    )
    key_rot = rotate(key_proj * key_scale * key_gain, cosine, sine_table).astype(jnp.bfloat16)
    attended, logsum = attention_forward(query_rot, key_rot, value_half, allowed)
    attn_flat = ring.tie(attended.reshape(token_count, -1))
    head_part = jnp.dot(attn_flat, w_out, preferred_element_type=jnp.float32)
    hidden = inputs + sum_heads(head_part, mp_count)
    scale_mid = rms_scale(hidden)
    weights = ring.result()
    normed_mid = (hidden * scale_mid * ffn_gain).astype(jnp.bfloat16)
    both = jnp.dot(normed_mid, weights[:, : 2 * mid_width], preferred_element_type=jnp.float32)
    gate_proj = both[:, :mid_width]
    up_proj = both[:, mid_width:]
    sig_gate = jax.nn.sigmoid(gate_proj)
    activated = (gate_proj * sig_gate * up_proj).astype(jnp.bfloat16)
    w_back = weights[:, 2 * mid_width :]
    d_act = jnp.dot(grad_out, w_back, preferred_element_type=jnp.float32)
    d_up = (d_act * gate_proj * sig_gate).astype(jnp.bfloat16)
    d_gate = (d_act * up_proj * sig_gate * (1.0 + gate_proj * (1.0 - sig_gate))).astype(
        jnp.bfloat16
    )
    d_both = jnp.concatenate([d_gate, d_up], axis=1)
    mlp_terms = jnp.concatenate(
        [
            lax.dot_general(
                normed_mid, d_both, down_rows, preferred_element_type=jnp.float32
            ).astype(jnp.bfloat16),
            lax.dot_general(
                grad_out, activated, down_rows, preferred_element_type=jnp.float32
            ).astype(jnp.bfloat16),
        ],
        axis=1,
    )
    d_mid_part = lax.dot_general(
        d_both, weights[:, : 2 * mid_width], across, preferred_element_type=jnp.float32
    )
    mlp_sum = Scatter(mlp_terms, dp_count)
    d_mid = sum_heads(d_mid_part, mp_count, mlp_sum.tie)
    ffn_part = lax.dot_general(activated, w_back, across, preferred_element_type=jnp.float32)
    output = (hidden + sum_heads(ffn_part, mp_count)).astype(jnp.bfloat16)
    g_ffn_gain = jnp.sum(d_mid_part * hidden * scale_mid, axis=0)
    d_hidden_norm, _ = norm_back(hidden, scale_mid, ffn_gain, d_mid)
    d_hidden = grad_out.astype(jnp.float32) + d_hidden_norm
    d_hidden_half = d_hidden.astype(jnp.bfloat16)
    g_out = lax.dot_general(d_hidden_half, attn_flat, down_rows, preferred_element_type=jnp.float32)
    d_attended = (
        lax.dot_general(d_hidden_half, w_out, across, preferred_element_type=jnp.float32)
        .astype(jnp.bfloat16)
        .reshape(token_count, -1, HEAD_DIM)
    )
    d_attended = mlp_sum.tie(d_attended)
    d_query_rot, d_key_rot, d_value = attention_backward(
        query_rot, key_rot, value_half, allowed, attended, logsum, d_attended
    )
    d_query_rot = mlp_sum.tie(d_query_rot)
    d_query, g_query_part = norm_back(
        query_proj, query_scale, query_gain, rotate_back(d_query_rot, cosine, sine_table)
    )
    d_key, g_key_part = norm_back(
        key_proj, key_scale, key_gain, rotate_back(d_key_rot, cosine, sine_table)
    )
    d_query_half = d_query.astype(jnp.bfloat16).reshape(token_count, -1)
    d_key_half = d_key.astype(jnp.bfloat16).reshape(token_count, -1)
    d_value_half = d_value.reshape(token_count, -1)
    d_heads = jnp.concatenate([d_query_half, d_key_half, d_value_half], axis=1)
    g_heads = lax.dot_general(normed_in, d_heads, down_rows, preferred_element_type=jnp.float32)
    d_in_part = lax.dot_general(d_heads, w_heads, across, preferred_element_type=jnp.float32)
    g_attn_gain = jnp.sum(d_in_part * inputs * scale_in, axis=0)
    vector = jnp.concatenate([g_attn_gain, g_ffn_gain, g_query_part, g_key_part])
    attn_terms = jnp.concatenate(
        [g_heads.astype(jnp.bfloat16), g_out.astype(jnp.bfloat16)], axis=1
    )
    attn_terms = mlp_sum.finished(attn_terms)
    if dp_count in (4, 8, 16) and mp_count == 4:
        attn_grads, d_in, gains = finish(attn_terms, d_in_part, vector, dp_count)
    else:
        attn_own = Scatter(attn_terms, dp_count).result().astype(jnp.bfloat16)
        attn_grads = Gather(attn_own, dp_count).result()
        gains = sum_all(vector, (("mp", mp_count), ("dp", dp_count)))
        d_in = sum_heads(d_in_part, mp_count)
    attn_grads = attn_grads.astype(jnp.float32)
    gains = jnp.split(gains, (width, 2 * width, 2 * width + HEAD_DIM))
    d_in_norm, _ = norm_back(inputs, scale_in, attn_gain, d_in)
    grad_tokens = d_hidden + d_in_norm
    mlp_grads = mlp_sum.result()
    value_at, out_at = query_width + key_width, query_width + 2 * key_width
    return (
        output,
        grad_tokens,
        gains[0],
        attn_grads[:, :query_width],
        attn_grads[:, query_width:value_at],
        attn_grads[:, value_at:out_at],
        gains[2],
        gains[3],
        attn_grads[:, out_at:].T,
        gains[1],
        mlp_grads[:, :mid_width],
        mlp_grads[:, mid_width : 2 * mid_width],
        mlp_grads[:, 2 * mid_width :].T,
    )


def solution(mesh):
    placed = (
        P("dp", None),
        P("dp", None),
        P(),
        P(None, "mp"),
        P(None, "mp"),
        P(None, "mp"),
        P(),
        P(),
        P("mp", None),
        P(),
        P("dp", "mp"),
        P("dp", "mp"),
        P("mp", "dp"),
        P("dp", None),
    )
    return jax.shard_map(
        functools.partial(shards, mesh.shape["dp"], mesh.shape["mp"]),
        mesh=mesh,
        in_specs=placed,
        out_specs=(
            P("dp", None),
            P("dp", None),
            P(),
            P(None, "mp"),
            P(None, "mp"),
            P(None, "mp"),
            P(),
            P(),
            P("mp", None),
            P(),
            P("dp", "mp"),
            P("dp", "mp"),
            P("mp", "dp"),
        ),
        check_vma=False,
    )
```

```python
import functools
import math

import jax
import jax.numpy as jnp
from jax import lax
from jax.experimental import pallas as pl
from jax.experimental.pallas import tpu as pltpu
from jax.sharding import PartitionSpec as P

HEAD_DIM = 64


EPS = 1e-05
ROPE_BASE = 1000000.0


def rms_scale(values):
    return lax.rsqrt(jnp.mean(values * values, axis=-1, keepdims=True) + EPS)


def norm_back(values, scale_fac, gain_vec, grad_normed):
    weighted = grad_normed * gain_vec
    grad_values = scale_fac * weighted - values * scale_fac * scale_fac * scale_fac * jnp.mean(
        weighted * values, axis=-1, keepdims=True
    )
    grad_gain = jnp.sum((grad_normed * values * scale_fac).reshape(-1, values.shape[-1]), axis=0)
    return (grad_values, grad_gain)


def segment_layout(segment_row):
    token_count = segment_row.shape[0]
    token_index = jnp.arange(token_count, dtype=jnp.int32)
    same_doc = segment_row[:, None] == segment_row[None, :]
    starts = jnp.min(jnp.where(same_doc, token_index[None, :], token_count), axis=1)
    allowed = same_doc & (token_index[None, :] <= token_index[:, None])
    return ((token_index - starts).astype(jnp.float32), allowed)


def rotary_tables(position, head_width):
    half_index = jnp.arange(head_width // 2, dtype=jnp.float32)
    frequency = ROPE_BASE ** (-2.0 * half_index / head_width)
    angles = position[:, None] * frequency[None, :]
    return (jnp.cos(angles)[:, None, :], jnp.sin(angles)[:, None, :])


def rotate(values, cosine, sine_table):
    half_width = values.shape[-1] // 2
    front_part = values[..., :half_width]
    back_part = values[..., half_width:]
    return jnp.concatenate(
        [
            front_part * cosine - back_part * sine_table,
            back_part * cosine + front_part * sine_table,
        ],
        axis=-1,
    )


def rotate_back(grads_in, cosine, sine_table):
    half_width = grads_in.shape[-1] // 2
    front_part = grads_in[..., :half_width]
    back_part = grads_in[..., half_width:]
    return jnp.concatenate(
        [
            front_part * cosine + back_part * sine_table,
            back_part * cosine - front_part * sine_table,
        ],
        axis=-1,
    )


def masked_scores(query_rot, key_rot, allowed):
    token_count, head_count, head_width = query_rot.shape
    group_count = key_rot.shape[1]
    grouped = query_rot.reshape(token_count, group_count, head_count // group_count, head_width)
    scores = jnp.einsum("qgrd,kgd->grqk", grouped, key_rot, preferred_element_type=jnp.float32) * (
        1.0 / math.sqrt(head_width)
    )
    return (jnp.where(allowed, scores, -1e30), grouped)


def attention_forward(query_rot, key_rot, value_half, allowed):
    token_count, head_count, head_width = query_rot.shape
    scores, grouped = masked_scores(query_rot, key_rot, allowed)
    row_peak = jnp.max(scores, axis=-1, keepdims=True)
    raised = jnp.exp(scores - row_peak)
    row_total = jnp.sum(raised, axis=-1, keepdims=True)
    logsum = row_peak + jnp.log(row_total)
    prob_half = (raised / row_total).astype(jnp.bfloat16)
    attended = jnp.einsum(
        "grqk,kgd->qgrd", prob_half, value_half, preferred_element_type=jnp.float32
    ).astype(jnp.bfloat16)
    return (attended.reshape(token_count, head_count, head_width), logsum)


def attention_backward(query_rot, key_rot, value_half, allowed, attended, logsum, d_attended):
    token_count, head_count, head_width = query_rot.shape
    group_count = key_rot.shape[1]
    scores, grouped = masked_scores(query_rot, key_rot, allowed)
    probs = jnp.where(allowed, jnp.exp(scores - logsum), 0.0)
    prob_half = probs.astype(jnp.bfloat16)
    d_grouped = d_attended.reshape(token_count, group_count, head_count // group_count, head_width)
    d_value = jnp.einsum(
        "grqk,qgrd->kgd", prob_half, d_grouped, preferred_element_type=jnp.float32
    ).astype(jnp.bfloat16)
    d_probs = jnp.einsum(
        "qgrd,kgd->grqk", d_grouped, value_half, preferred_element_type=jnp.float32
    )
    row_delta = jnp.sum(d_attended.astype(jnp.float32) * attended.astype(jnp.float32), axis=-1)
    row_delta = row_delta.reshape(token_count, group_count, head_count // group_count).transpose(
        1, 2, 0
    )[..., None]
    d_scores = (probs * (d_probs - row_delta) * (1.0 / math.sqrt(head_width))).astype(jnp.bfloat16)
    d_query_rot = jnp.einsum(
        "grqk,kgd->qgrd", d_scores, key_rot, preferred_element_type=jnp.float32
    ).reshape(token_count, head_count, head_width)
    d_key_rot = jnp.einsum("grqk,qgrd->kgd", d_scores, grouped, preferred_element_type=jnp.float32)
    return (d_query_rot, d_key_rot, d_value)


RING_LIMIT = 16


def ring_order(count):
    return tuple(range(0, count, 2)) + tuple(range(count - 1, 0, -2))


def ring_moves(count):
    order = ring_order(count)
    ahead = [(order[i], order[(i + 1) % count]) for i in range(count)]
    back = [(order[(i + 1) % count], order[i]) for i in range(count)]
    return ahead, back


def ring_place(count):
    order = ring_order(count)
    place = [0] * count
    for spot, owner in enumerate(order):
        place[owner] = spot
    me = jnp.array(place, dtype=jnp.int32)[lax.axis_index("dp")]
    table = jnp.array(order, dtype=jnp.int32)
    return lambda step: table[(me + step + 2 * count) % count]


class Gather:
    def __init__(self, block, count):
        self.count, self.block = count, block
        self.ring = count >= 4 and count % 2 == 0 and count <= RING_LIMIT
        self.left = self.right = block
        self.done = 0
        if self.ring:
            self.owner = ring_place(count)
            self.moves = ring_moves(count)
            self.whole = None

    def put(self, piece, who, shift=0):
        start = who * self.block.shape[0] + shift
        self.whole = lax.dynamic_update_slice_in_dim(self.whole, piece, start, 0)

    def step(self):
        if not self.ring or self.done >= self.count // 2:
            return
        self.done += 1
        ahead, back = self.moves
        half = self.block.shape[0] // 2
        if self.done < self.count // 2:
            self.left = lax.ppermute(self.left, "dp", ahead)
            self.right = lax.ppermute(self.right, "dp", back)
            if self.whole is None:
                zero, self.left, self.right = lax.optimization_barrier(
                    (jnp.zeros((), self.block.dtype), self.left, self.right)
                )
                self.whole = jnp.broadcast_to(
                    zero, (self.count * self.block.shape[0],) + self.block.shape[1:]
                )
                self.put(self.block, self.owner(0))
            self.put(self.left, self.owner(-self.done))
            self.put(self.right, self.owner(self.done))
        else:
            far = self.owner(self.done)
            self.put(lax.ppermute(self.left[:half], "dp", ahead), far)
            self.put(lax.ppermute(self.right[half:], "dp", back), far, half)

    def tie(self, value):
        if not self.ring:
            return value
        value, self.left, self.right = lax.optimization_barrier((value, self.left, self.right))
        self.step()
        return value

    def result(self):
        if self.count == 1:
            return self.block
        if not self.ring:
            return lax.all_gather(self.block, "dp", axis=0, tiled=True)
        while self.done < self.count // 2:
            self.step()
        return self.whole


class Scatter:
    def __init__(self, terms, count):
        self.count, self.terms = count, terms
        self.ring = count >= 4 and count % 2 == 0 and count <= RING_LIMIT
        if not self.ring:
            return
        self.rows = terms.shape[0] // count
        self.owner = ring_place(count)
        self.moves = ring_moves(count)
        self.left = count // 2
        half = self.rows // 2
        self.cw = self.term(self.left, 0, half)
        self.ccw = self.term(self.left, half, half)
        self.send()

    def term(self, step, start=0, size=None):
        return lax.dynamic_slice_in_dim(
            self.terms, self.owner(step) * self.rows + start, size or self.rows, 0
        )

    def plus(self, one, two):
        return (one.astype(jnp.float32) + two.astype(jnp.float32)).astype(self.terms.dtype)

    def send(self):
        self.cw = lax.ppermute(self.cw, "dp", self.moves[0])
        self.ccw = lax.ppermute(self.ccw, "dp", self.moves[1])
        self.left -= 1

    def step(self):
        if not self.ring or self.left == 0:
            return
        step, half = self.left, self.rows // 2
        if step == self.count // 2 - 1:
            self.cw = jnp.concatenate(
                [self.plus(self.term(step, 0, half), self.cw), self.term(step, half, half)], axis=0
            )
            self.ccw = jnp.concatenate(
                [self.term(-step, 0, half), self.plus(self.term(-step, half, half), self.ccw)],
                axis=0,
            )
        else:
            self.cw = self.plus(self.term(step), self.cw)
            self.ccw = self.plus(self.term(-step), self.ccw)
        self.send()

    def tie(self, value):
        if not self.ring or self.left == 0:
            return value
        value, self.cw, self.ccw = lax.optimization_barrier((value, self.cw, self.ccw))
        self.step()
        return value

    def result(self):
        if self.count == 1:
            return self.terms.astype(jnp.float32)
        if not self.ring:
            total = lax.psum_scatter(self.terms, "dp", scatter_dimension=0, tiled=True)
            return total.astype(jnp.float32)
        while self.left:
            self.step()
        own = self.term(0).astype(jnp.float32)
        return own + self.cw.astype(jnp.float32) + self.ccw.astype(jnp.float32)


def sum_all(vector, sizes):
    for name, count in sizes:
        if count & (count - 1) or count > RING_LIMIT:
            vector = lax.psum(vector, name)
            continue
        reach = 1
        while reach < count:
            pairs = [(i, i ^ reach) for i in range(count)]
            vector = vector + lax.ppermute(vector, name, pairs)
            reach *= 2
    return vector


def sum_heads(part, count, tie=lambda value: value):
    if count != 4:
        return lax.psum(part, "mp")
    near = [(i, i ^ 1) for i in range(count)]
    across = [(i, i ^ 2) for i in range(count)]
    half = part.shape[0] // 2
    bit = lax.axis_index("mp") % 2
    kept = lax.dynamic_slice_in_dim(part, bit * half, half, 0)
    given = lax.dynamic_slice_in_dim(part, (1 - bit) * half, half, 0).astype(jnp.bfloat16)
    mine = kept + lax.ppermute(given, "mp", near).astype(jnp.float32)
    mine = tie(lax.reduce_precision(mine, 8, 7))
    other = lax.ppermute(mine.astype(jnp.bfloat16), "mp", across)
    mine = mine + other.astype(jnp.float32)
    other = lax.ppermute(mine, "mp", near)
    return jnp.where(
        bit == 0,
        jnp.concatenate([mine, other], axis=0),
        jnp.concatenate([other, mine], axis=0),
    )


MESH_ID = pl.DeviceIdType.MESH


def finish_kernel(
    count,
    terms,
    part,
    vector,
    grads,
    total,
    gains,
    cw_in,
    ccw_in,
    cw_out,
    ccw_out,
    near_out,
    near_in,
    far_out,
    far_in,
    vec_out,
    vec_in,
    ring_send,
    ring_recv,
    pair_send,
    pair_recv,
    vec_send,
    vec_recv,
):
    dp, mp = lax.axis_index("dp"), lax.axis_index("mp")
    rows = terms.shape[0] // count
    half = rows // 2
    far = count // 2

    def owner(spot):
        spot = lax.rem(spot + 2 * count, count)
        low = 1 - spot // far
        return low * 2 * spot + (1 - low) * (2 * (count - spot) - 1)

    odd = lax.rem(dp, 2)
    place = (1 - odd) * (dp // 2) + odd * (count - (dp + 1) // 2)
    ahead, behind = (owner(place + 1), mp), (owner(place - 1), mp)

    def pair(value, reach):
        return value + reach * (1 - 2 * lax.rem(value // reach, 2))

    partners = [(dp, pair(mp, 1)), (dp, pair(mp, 2))]
    reach = 1
    while reach < count:
        partners.append((pair(dp, reach), mp))
        reach *= 2

    barrier = pltpu.get_barrier_semaphore()
    for target in [ahead, behind] + partners:
        pl.semaphore_signal(barrier, inc=1, device_id=target, device_id_type=MESH_ID)
    pl.semaphore_wait(barrier, 2 + len(partners))

    def send(source, dest, sems, target):
        copy = pltpu.make_async_remote_copy(
            src_ref=source,
            dst_ref=dest,
            send_sem=sems[0],
            recv_sem=sems[1],
            device_id=target,
            device_id_type=MESH_ID,
        )
        copy.start()
        return copy

    def rows_of(spot, start=0, size=None):
        return pl.ds(pl.multiple_of(owner(place + spot) * rows + start, 16), size or rows)

    def term(spot, start=0, size=None):
        return terms[rows_of(spot, start, size), :].astype(jnp.float32)

    def ring_sems(way, turn):
        return ring_send.at[way, turn], ring_recv.at[way, turn]

    cw = send(
        terms.at[rows_of(far, 0, half), :], cw_in.at[0, pl.ds(0, half)], ring_sems(0, 0), ahead
    )
    ccw = send(
        terms.at[rows_of(-far, half, half), :],
        ccw_in.at[0, pl.ds(half, half)],
        ring_sems(1, 0),
        behind,
    )

    bit = lax.rem(mp, 2)
    middle = part.shape[0] // 2
    kept = pl.ds(pl.multiple_of(bit * middle, 16), middle)
    given = pl.ds(pl.multiple_of((1 - bit) * middle, 16), middle)
    near_out[...] = part[given, :].astype(jnp.bfloat16)
    pairs = [send(near_out, near_in, (pair_send.at[0], pair_recv.at[0]), partners[0])]

    vec_out[0] = vector[...]
    vecs = [send(vec_out.at[0], vec_in.at[0], (vec_send.at[0], vec_recv.at[0]), partners[0])]

    def vector_turn():
        turn = len(vecs) - 1
        if turn >= len(partners):
            return
        vecs[turn].wait()
        both = vec_out[turn] + vec_in[turn]
        if turn + 1 == len(partners):
            gains[...] = both
            vecs.append(None)
            return
        vec_out[turn + 1] = both
        sems = (vec_send.at[turn + 1], vec_recv.at[turn + 1])
        vecs.append(send(vec_out.at[turn + 1], vec_in.at[turn + 1], sems, partners[turn + 1]))

    def pair_turn():
        turn = len(pairs)
        if turn == 1:
            pairs[0].wait()
            far_out[...] = (part[kept, :] + near_in[...].astype(jnp.float32)).astype(jnp.bfloat16)
            pairs.append(send(far_out, far_in, (pair_send.at[1], pair_recv.at[1]), partners[1]))
        elif turn == 2:
            pairs[1].wait()
            total[kept, :] = far_out[...].astype(jnp.float32) + far_in[...].astype(jnp.float32)
            view = total.at[kept, :]
            pairs.append(send(view, view, (pair_send.at[2], pair_recv.at[2]), partners[0]))
        elif turn == 3:
            pairs[2].wait()
            pairs.append(None)

    for turn in range(1, far):
        spot = far - turn
        cw.wait()
        if turn == 1:
            low, high = pl.ds(0, half), pl.ds(half, half)
            cw_out[0, low] = (term(spot, 0, half) + cw_in[0, low].astype(jnp.float32)).astype(
                jnp.bfloat16
            )
            cw_out[0, high] = terms[rows_of(spot, half, half), :]
        else:
            cw_out[turn - 1] = (term(spot) + cw_in[turn - 1].astype(jnp.float32)).astype(
                jnp.bfloat16
            )
        cw = send(cw_out.at[turn - 1], cw_in.at[turn], ring_sems(0, turn), ahead)
        ccw.wait()
        if turn == 1:
            ccw_out[0, high] = (
                term(-spot, half, half) + ccw_in[0, high].astype(jnp.float32)
            ).astype(jnp.bfloat16)
            ccw_out[0, low] = terms[rows_of(-spot, 0, half), :]
        else:
            ccw_out[turn - 1] = (term(-spot) + ccw_in[turn - 1].astype(jnp.float32)).astype(
                jnp.bfloat16
            )
        ccw = send(ccw_out.at[turn - 1], ccw_in.at[turn], ring_sems(1, turn), behind)
        pair_turn()
        vector_turn()
    cw.wait()
    ccw.wait()
    own = term(0) + cw_in[far - 1].astype(jnp.float32) + ccw_in[far - 1].astype(jnp.float32)
    grads[rows_of(0), :] = own.astype(jnp.bfloat16)

    for turn in range(1, far + 1):
        size = rows if turn < far else half
        shift = 0 if turn < far else half
        one = grads.at[rows_of(1 - turn, 0, size), :]
        two = grads.at[rows_of(turn - 1, shift, size), :]
        cw = send(one, one, ring_sems(0, far + turn - 1), ahead)
        ccw = send(two, two, ring_sems(1, far + turn - 1), behind)
        pair_turn()
        vector_turn()
        cw.wait()
        ccw.wait()
    while len(pairs) < 4:
        pair_turn()
    while len(vecs) <= len(partners):
        vector_turn()


def finish(terms, part, vector, dp_count):
    rows, columns = terms.shape[0] // dp_count, terms.shape[1]
    far, steps = dp_count // 2, 2 + dp_count.bit_length() - 1
    lanes = 128
    tall = -(-vector.shape[0] // (8 * lanes)) * 8
    padded = jnp.pad(vector, (0, tall * lanes - vector.shape[0])).reshape(tall, lanes)
    middle = (part.shape[0] // 2, part.shape[1])
    ring_slots = pltpu.VMEM((far, rows, columns), jnp.bfloat16)
    half_slot = pltpu.VMEM(middle, jnp.bfloat16)
    vec_slots = pltpu.VMEM((steps, tall, lanes), jnp.float32)
    vmem = pl.BlockSpec(memory_space=pltpu.VMEM)
    grads, total, gains = pl.pallas_call(
        functools.partial(finish_kernel, dp_count),
        out_shape=(
            jax.ShapeDtypeStruct(terms.shape, jnp.bfloat16),
            jax.ShapeDtypeStruct(part.shape, jnp.float32),
            jax.ShapeDtypeStruct(padded.shape, jnp.float32),
        ),
        in_specs=[vmem] * 3,
        out_specs=(vmem,) * 3,
        scratch_shapes=[ring_slots] * 4
        + [half_slot] * 4
        + [vec_slots] * 2
        + [pltpu.SemaphoreType.DMA((2, 2 * far))] * 2
        + [pltpu.SemaphoreType.DMA((3,))] * 2
        + [pltpu.SemaphoreType.DMA((steps,))] * 2,
        compiler_params=pltpu.CompilerParams(
            collective_id=0, has_side_effects=True, vmem_limit_bytes=24 * 1024 * 1024
        ),
    )(terms, part, padded)
    return grads, total, gains.reshape(-1)[: vector.shape[0]]


def shards(
    dp_count,
    mp_count,
    tokens,
    segment_ids,
    attn_gain,
    w_query,
    w_key,
    w_value,
    query_gain,
    key_gain,
    w_out,
    ffn_gain,
    w_gate,
    w_up,
    w_down,
    grad_out,
):
    token_count, width = tokens.shape
    across = (((1,), (1,)), ((), ()))
    down_rows = (((0,), (0,)), ((), ()))
    mid_width = w_gate.shape[1]
    block = jnp.concatenate([w_gate, w_up, w_down.T], axis=1)
    tokens, block = lax.optimization_barrier((tokens, block))
    ring = Gather(block, dp_count)
    ring.step()
    w_heads = jnp.concatenate([w_query, w_key, w_value], axis=1)
    query_width, key_width = w_query.shape[1], w_key.shape[1]
    inputs = tokens.astype(jnp.float32)
    scale_in = rms_scale(inputs)
    normed_in = (inputs * scale_in * attn_gain).astype(jnp.bfloat16)
    heads_proj = jnp.dot(normed_in, w_heads, preferred_element_type=jnp.float32)
    query_proj = heads_proj[:, :query_width].reshape(token_count, -1, HEAD_DIM)
    key_proj = heads_proj[:, query_width : query_width + key_width].reshape(
        token_count, -1, HEAD_DIM
    )
    value_half = (
        heads_proj[:, query_width + key_width :]
        .astype(jnp.bfloat16)
        .reshape(token_count, -1, HEAD_DIM)
    )
    query_scale = rms_scale(query_proj)
    key_scale = rms_scale(key_proj)
    position, allowed = segment_layout(segment_ids[0])
    cosine, sine_table = rotary_tables(position, HEAD_DIM)
    query_rot = rotate(query_proj * query_scale * query_gain, cosine, sine_table).astype(
        jnp.bfloat16
    )
    key_rot = rotate(key_proj * key_scale * key_gain, cosine, sine_table).astype(jnp.bfloat16)
    attended, logsum = attention_forward(query_rot, key_rot, value_half, allowed)
    attn_flat = ring.tie(attended.reshape(token_count, -1))
    head_part = jnp.dot(attn_flat, w_out, preferred_element_type=jnp.float32)
    hidden = inputs + sum_heads(head_part, mp_count)
    scale_mid = rms_scale(hidden)
    weights = ring.result()
    normed_mid = (hidden * scale_mid * ffn_gain).astype(jnp.bfloat16)
    both = jnp.dot(normed_mid, weights[:, : 2 * mid_width], preferred_element_type=jnp.float32)
    gate_proj = both[:, :mid_width]
    up_proj = both[:, mid_width:]
    sig_gate = jax.nn.sigmoid(gate_proj)
    activated = (gate_proj * sig_gate * up_proj).astype(jnp.bfloat16)
    w_back = weights[:, 2 * mid_width :]
    d_act = jnp.dot(grad_out, w_back, preferred_element_type=jnp.float32)
    d_up = (d_act * gate_proj * sig_gate).astype(jnp.bfloat16)
    d_gate = (d_act * up_proj * sig_gate * (1.0 + gate_proj * (1.0 - sig_gate))).astype(
        jnp.bfloat16
    )
    d_both = jnp.concatenate([d_gate, d_up], axis=1)
    mlp_terms = jnp.concatenate(
        [
            lax.dot_general(
                normed_mid, d_both, down_rows, preferred_element_type=jnp.float32
            ).astype(jnp.bfloat16),
            lax.dot_general(
                grad_out, activated, down_rows, preferred_element_type=jnp.float32
            ).astype(jnp.bfloat16),
        ],
        axis=1,
    )
    d_mid_part = lax.dot_general(
        d_both, weights[:, : 2 * mid_width], across, preferred_element_type=jnp.float32
    )
    mlp_sum = Scatter(mlp_terms, dp_count)
    d_mid = sum_heads(d_mid_part, mp_count, mlp_sum.tie)
    ffn_part = lax.dot_general(activated, w_back, across, preferred_element_type=jnp.float32)
    output = (hidden + sum_heads(ffn_part, mp_count)).astype(jnp.bfloat16)
    g_ffn_gain = jnp.sum(d_mid_part * hidden * scale_mid, axis=0)
    d_hidden_norm, _ = norm_back(hidden, scale_mid, ffn_gain, d_mid)
    d_hidden = grad_out.astype(jnp.float32) + d_hidden_norm
    d_hidden_half = d_hidden.astype(jnp.bfloat16)
    g_out = lax.dot_general(d_hidden_half, attn_flat, down_rows, preferred_element_type=jnp.float32)
    d_attended = (
        lax.dot_general(d_hidden_half, w_out, across, preferred_element_type=jnp.float32)
        .astype(jnp.bfloat16)
        .reshape(token_count, -1, HEAD_DIM)
    )
    d_attended = mlp_sum.tie(d_attended)
    d_query_rot, d_key_rot, d_value = attention_backward(
        query_rot, key_rot, value_half, allowed, attended, logsum, d_attended
    )
    d_query_rot = mlp_sum.tie(d_query_rot)
    d_query, g_query_part = norm_back(
        query_proj, query_scale, query_gain, rotate_back(d_query_rot, cosine, sine_table)
    )
    d_key, g_key_part = norm_back(
        key_proj, key_scale, key_gain, rotate_back(d_key_rot, cosine, sine_table)
    )
    d_query_half = d_query.astype(jnp.bfloat16).reshape(token_count, -1)
    d_key_half = d_key.astype(jnp.bfloat16).reshape(token_count, -1)
    d_value_half = d_value.reshape(token_count, -1)
    mlp_grads = mlp_sum.result()
    d_heads = jnp.concatenate([d_query_half, d_key_half, d_value_half], axis=1)
    g_heads = lax.dot_general(normed_in, d_heads, down_rows, preferred_element_type=jnp.float32)
    d_in_part = lax.dot_general(d_heads, w_heads, across, preferred_element_type=jnp.float32)
    g_attn_gain = jnp.sum(d_in_part * inputs * scale_in, axis=0)
    vector = jnp.concatenate([g_attn_gain, g_ffn_gain, g_query_part, g_key_part])
    attn_terms = jnp.concatenate(
        [g_heads.astype(jnp.bfloat16), g_out.astype(jnp.bfloat16)], axis=1
    )
    if dp_count in (4, 8, 16) and mp_count == 4:
        attn_grads, d_in, gains = finish(attn_terms, d_in_part, vector, dp_count)
    else:
        attn_own = Scatter(attn_terms, dp_count).result().astype(jnp.bfloat16)
        attn_grads = Gather(attn_own, dp_count).result()
        gains = sum_all(vector, (("mp", mp_count), ("dp", dp_count)))
        d_in = sum_heads(d_in_part, mp_count)
    attn_grads = attn_grads.astype(jnp.float32)
    gains = jnp.split(gains, (width, 2 * width, 2 * width + HEAD_DIM))
    d_in_norm, _ = norm_back(inputs, scale_in, attn_gain, d_in)
    grad_tokens = d_hidden + d_in_norm
    value_at, out_at = query_width + key_width, query_width + 2 * key_width
    return (
        output,
        grad_tokens,
        gains[0],
        attn_grads[:, :query_width],
        attn_grads[:, query_width:value_at],
        attn_grads[:, value_at:out_at],
        gains[2],
        gains[3],
        attn_grads[:, out_at:].T,
        gains[1],
        mlp_grads[:, :mid_width],
        mlp_grads[:, mid_width : 2 * mid_width],
        mlp_grads[:, 2 * mid_width :].T,
    )


def solution(mesh):
    placed = (
        P("dp", None),
        P("dp", None),
        P(),
        P(None, "mp"),
        P(None, "mp"),
        P(None, "mp"),
        P(),
        P(),
        P("mp", None),
        P(),
        P("dp", "mp"),
        P("dp", "mp"),
        P("mp", "dp"),
        P("dp", None),
    )
    return jax.shard_map(
        functools.partial(shards, mesh.shape["dp"], mesh.shape["mp"]),
        mesh=mesh,
        in_specs=placed,
        out_specs=(
            P("dp", None),
            P("dp", None),
            P(),
            P(None, "mp"),
            P(None, "mp"),
            P(None, "mp"),
            P(),
            P(),
            P("mp", None),
            P(),
            P("dp", "mp"),
            P("dp", "mp"),
            P("mp", "dp"),
        ),
        check_vma=False,
    )
```
